32 devices in a mesh: outer: 8 (over z, y), inner: 4 (over x, core).
Axes of the slice: x: 2, y: 2, z: 4, core: 2. Of those that a mesh axis runs over, the one named last changes fastest.
Arguments:
- hidden_in: bfloat16 [65536, 1024], P(('outer', 'inner')), may hold values from -6 to 6
- segment_ids: int32 [65536], P(('outer', 'inner')), may hold values from 0 to 15, never falling along the last dimension, each value on 1 to 16384 neighbouring positions
- query_weight: bfloat16 [1024, 1024], replicated, may hold values from -0.1875 to 0.1875
- key_weight: bfloat16 [1024, 1024], replicated, may hold values from -0.1875 to 0.1875
- value_weight: bfloat16 [1024, 1024], replicated, may hold values from -0.1875 to 0.1875
- output_weight: bfloat16 [1024, 1024], replicated, may hold values from -0.1875 to 0.1875
- head_gain: float32 [1024], replicated, may hold values from 0.1 to 1.9
Outputs:
- layer_out: bfloat16 [65536, 1024], P(('outer', 'inner'))
The draws below stay inside these ranges and needn't reach their ends.
Inputs may be any that keep to these rules, and one draw needn't show every extreme that they name: `segment_ids`: ids never fall along the window; each history spans 1 to 16384 tokens and one spans exactly 16384.
All inputs are finite; a program needn't handle non-finite values.
Results may differ from the reference program's by a relative error of at most 0.011.
Values sent between devices are 32-bit elements; how exact they have to be, the bound alone decides.
A program may use at most 256 MiB of HBM per device.

```python
import math
import jax
import jax.numpy as jnp
import numpy as np
from jax import lax

D = 1024
H = 8
HD = 128
BLK = 512
TOKENS = 65536
COUNT = 16
MOST_LEN = 16384


def level_of(own_key, extent, cuts, low, largest):
    factor_of, own = 1.0, jax.random.fold_in(own_key, 6)
    for dim, blocks in cuts:
        steps = jnp.exp(jax.random.uniform(jax.random.fold_in(own, dim), (blocks,), jnp.float32, low / len(cuts), largest / len(cuts)))
        factor_of = factor_of * jnp.repeat(steps, extent[dim] // blocks).reshape([-1 if axis == dim else 1 for axis in range(len(extent))])
    return factor_of


def length_profile(count, total, reach, skew):
    weights = [(1 << 20) // math.isqrt(grade ** skew) + 1 for grade in range(2, count + 1)]
    surplus, counts = total - reach - (count - 1), [1] * (count - 1)
    while surplus > 0:
        free = [i for i in range(count - 1) if counts[i] < reach]
        whole, remaining = sum([weights[i] for i in free]), surplus
        for i in free:
            addition = min(reach - counts[i], max(1, remaining * weights[i] // whole), surplus)
            counts[i] = counts[i] + addition
            surplus = surplus - addition
    return np.array([reach] + counts)


def uneven_parts(rng, amount, total, bound, lean):
    if amount == 2:
        one = jax.random.randint(rng, (), max(1, total - bound), min(bound, total - 1) + 1)
        return jnp.stack([one, total - one])
    tallies = jnp.asarray(length_profile(amount, total, bound, lean), jnp.int32)
    pairs = (amount - 1) // 2
    donor, taker = tallies[1:1 + 2 * pairs:2], tallies[2:2 + 2 * pairs:2]
    room = jnp.minimum(donor - 1, bound - taker)
    shifted = jax.random.randint(jax.random.fold_in(rng, 1), (pairs,), 0, 1 << 20) % (room + 1)
    tallies = tallies.at[1:1 + 2 * pairs:2].set(donor - shifted).at[2:2 + 2 * pairs:2].set(taker + shifted)
    return tallies[jax.random.permutation(jax.random.fold_in(rng, 2), amount)]


def centred(rng, extent, width, limit, shards=(), kind=jnp.bfloat16):
    values = jax.random.normal(rng, extent, jnp.float32) * width
    if len(shards) > 0:
        values = level_of(rng, extent, shards, -0.22, 0.18) * values
    return jnp.clip(values, min=-limit, max=limit).astype(kind)


def setup_inputs(seed: int = 0) -> dict:
    arg_keys = jax.random.split(jax.random.key(seed), 8)
    hidden_in = centred(arg_keys[0], (TOKENS, D), 1.0, 6.0, ((0, 32),))
    segment_ids = jnp.searchsorted(jnp.cumsum(uneven_parts(arg_keys[1], COUNT, TOKENS, MOST_LEN, 2)), jnp.arange(TOKENS), side="right").astype(jnp.int32)
    query_weight = centred(arg_keys[2], (D, D), D ** -0.5, 0.1875)
    key_weight = centred(arg_keys[3], (D, D), D ** -0.5, 0.1875)
    value_weight = centred(arg_keys[4], (D, D), D ** -0.5, 0.1875)
    output_weight = centred(arg_keys[5], (D, D), D ** -0.5, 0.1875)
    head_gain = jnp.clip(1.0 + 0.18 * jax.random.normal(arg_keys[6], (D,), jnp.float32), 0.1, 1.9)
    return {"hidden_in": hidden_in, "segment_ids": segment_ids, "query_weight": query_weight, "key_weight": key_weight, "value_weight": value_weight, "output_weight": output_weight, "head_gain": head_gain}


def reference(hidden_in, segment_ids, query_weight, key_weight, value_weight, output_weight, head_gain):
    total = hidden_in.shape[0]
    queries = jnp.dot(hidden_in, query_weight, preferred_element_type=jnp.float32).astype(jnp.bfloat16)
    keys = jnp.dot(hidden_in, key_weight, preferred_element_type=jnp.float32).astype(jnp.bfloat16)
    values = jnp.dot(hidden_in, value_weight, preferred_element_type=jnp.float32).astype(jnp.bfloat16)
    blocks = total // BLK
    q_blocks = queries.reshape(blocks, BLK, H, HD)
    k_blocks = keys.reshape(blocks, BLK, H, HD)
    v_blocks = values.reshape(blocks, BLK, H, HD)
    id_blocks = segment_ids.reshape(blocks, BLK)
    causal = jnp.tril(jnp.ones((BLK, BLK), dtype=bool))

    def step(carry, block):
        state, last_id = carry
        q_b, k_b, v_b, i_b = block
        keep = causal & (i_b[:, None] == i_b[None, :])
        scores = jnp.einsum('shd,thd->hst', q_b.astype(jnp.float32), k_b.astype(jnp.float32))
        scores = jnp.where(keep[None], scores, 0.0).astype(jnp.bfloat16)
        local = jnp.einsum('hst,thd->shd', scores.astype(jnp.float32), v_b.astype(jnp.float32))
        carried = jnp.einsum('shd,hde->she', q_b.astype(jnp.float32), state, precision=lax.Precision.HIGHEST)
        carried = carried * (i_b == last_id).astype(jnp.float32)[:, None, None]
        tail = (i_b == i_b[-1]).astype(jnp.bfloat16)[:, None, None]
        contrib = jnp.einsum('thd,the->hde', (k_b * tail).astype(jnp.float32), v_b.astype(jnp.float32))
        held = (i_b[0] == i_b[-1]) & (i_b[0] == last_id)
        state = jnp.where(held, state, jnp.zeros_like(state)) + contrib
        return ((state, i_b[-1]), local + carried)
    init = (jnp.zeros((H, HD, HD), jnp.float32), jnp.array(-1, dtype=jnp.int32))
    _, mixed = lax.scan(step, init, (q_blocks, k_blocks, v_blocks, id_blocks))
    mixed = mixed.reshape(total, H, HD)
    scale = lax.rsqrt(lax.optimization_barrier(jnp.mean(mixed * mixed, axis=-1, keepdims=True)) + 1e-06)
    normed = (mixed * scale * head_gain.reshape(H, HD)).astype(jnp.bfloat16).reshape(total, D)
    return jnp.dot(normed, output_weight, preferred_element_type=jnp.float32).astype(jnp.bfloat16)
```

```python
import functools

import jax
import jax.numpy as jnp
from jax import lax
from jax.experimental import pallas as pl
from jax.experimental.pallas import tpu as pltpu
from jax.sharding import PartitionSpec as P

D = 1024
H = 8
HD = 128
MOST_LEN = 16384
TILE = 512
CH = 256
MSG = HD + 8
MESH = pl.DeviceIdType.MESH
F32 = jnp.float32
BF16 = jnp.bfloat16


def dot(a, b):
    return jnp.dot(a, b, preferred_element_type=F32)


def kernel(
    n_outer, n_inner, group,
    ids, gain, hid_hbm, wq_hbm, wk_hbm, wv_hbm, wo_hbm, out_hbm,
    hid, wq, wk, wv, wo, qs, ks, vs, loc, outv, idc, st, sb, cb,
    msg1, got1, tail, prev, msg3, got3,
    hid_sem, w_sem, out_sem, s1, r1, s2, r2, s3, r3,
):
    tokens = hid.shape[0]
    tiles = tokens // TILE
    per = TILE // CH
    total = n_outer * n_inner
    groups = total // group
    me = lax.axis_index("outer") * n_inner + lax.axis_index("inner")
    g = me // group
    m = me % group

    def at(index):
        return (index // n_inner, index % n_inner)

    def peer(d):
        return (m + d) % group

    def hid_copy(i):
        rows = pl.ds(pl.multiple_of(i * TILE, TILE), TILE)
        return pltpu.make_async_copy(hid_hbm.at[rows], hid.at[rows], hid_sem.at[i])

    w_copies = [
        pltpu.make_async_copy(src, dst, w_sem.at[i])
        for i, (src, dst) in enumerate(((wk_hbm, wk), (wv_hbm, wv), (wq_hbm, wq), (wo_hbm, wo)))
    ]
    w_copies[0].start()
    hid_copy(0).start()
    w_copies[1].start()
    for i in range(1, tiles):
        hid_copy(i).start()
    w_copies[2].start()
    w_copies[3].start()

    barrier = pltpu.get_barrier_semaphore()
    for d in range(1, group):
        pl.semaphore_signal(barrier, inc=1, device_id=at(g * group + peer(d)), device_id_type=MESH)

    @pl.when(g > 0)
    def _():
        pl.semaphore_signal(barrier, inc=1, device_id=at(me - group), device_id_type=MESH)

    @pl.when(g < groups - 1)
    def _():
        pl.semaphore_signal(barrier, inc=1, device_id=at(me + group), device_id_type=MESH)

    for r in range(tokens // 128):
        row = ids[r : r + 1, :].astype(F32)
        idc[r * 128 : (r + 1) * 128, :] = jnp.transpose(jnp.broadcast_to(row, (128, 128)))
    st[...] = jnp.zeros_like(st)

    def last_of(c):
        return idc[pl.ds(pl.multiple_of(c * CH + CH - 8, 8), 8), :][7:8, :]

    def before(c):
        return idc[pl.ds(pl.multiple_of(jnp.maximum(c * CH - 8, 0), 8), 8), :][7:8, :]

    w_copies[0].wait()
    w_copies[1].wait()

    def project(i, carry):
        hid_copy(i).wait()
        rows = pl.ds(pl.multiple_of(i * TILE, TILE), TILE)
        x = hid[rows, :]
        ks[rows, :] = dot(x, wk[...]).astype(BF16)
        vs[rows, :] = dot(x, wv[...]).astype(BF16)
        for j in range(per):
            c = i * per + j
            part = pl.ds(pl.multiple_of(c * CH, CH), CH)
            last = last_of(c)
            held = last == before(c)
            mask = jnp.where(idc[part, :] == last, 1.0, 0.0).astype(BF16)
            for h in range(H):
                lanes = slice(h * HD, (h + 1) * HD)
                state = st[h]
                sb[c, h] = state.astype(BF16)
                add = lax.dot_general(
                    ks[part, lanes] * mask, vs[part, lanes], (((0,), (0,)), ((), ())),
                    preferred_element_type=F32,
                )
                st[h] = jnp.where(held, state, 0.0) + add
        return carry

    lax.fori_loop(0, tiles, project, 0)

    my_last = jnp.broadcast_to(last_of(tokens // CH - 1), (8, 128))
    for h in range(H):
        msg1[h, 0:HD, :] = st[h]
        msg1[h, HD:MSG, :] = my_last
    got1[pl.ds(m, 1)] = msg1[pl.ds(m, 1)]

    @pl.when(g == 0)
    def _():
        prev[0:HD, :] = jnp.zeros((HD, HD), F32)
        prev[HD:MSG, :] = jnp.full((8, HD), -1.0, F32)

    has_prev = jnp.where(g > 0, 1, 0)
    has_next = jnp.where(g < groups - 1, 1, 0)
    pl.semaphore_wait(barrier, group - 1 + has_prev + has_next)

    def copy1(d):
        return pltpu.make_async_remote_copy(
            src_ref=msg1.at[peer(d)], dst_ref=got1.at[m],
            send_sem=s1.at[d - 1], recv_sem=r1.at[d - 1],
            device_id=at(g * group + peer(d)), device_id_type=MESH,
        )

    def copy2():
        return pltpu.make_async_remote_copy(
            src_ref=tail, dst_ref=prev, send_sem=s2, recv_sem=r2,
            device_id=at(me + group), device_id_type=MESH,
        )

    def copy3(d):
        return pltpu.make_async_remote_copy(
            src_ref=msg3.at[peer(d)], dst_ref=got3.at[m],
            send_sem=s3.at[d - 1], recv_sem=r3.at[d - 1],
            device_id=at(g * group + peer(d)), device_id_type=MESH,
        )

    for d in range(1, group):
        copy1(d).start()

    def exchange_tail():
        for d in range(1, group):
            copy1(d).wait_recv()
        state = got1[0, 0:HD, :]
        for j in range(1, group):
            same = got1[j, HD : HD + 1, :] == got1[j - 1, HD : HD + 1, :]
            state = got1[j, 0:HD, :] + jnp.where(same, state, 0.0)
        tail[0:HD, :] = state
        tail[HD:MSG, :] = got1[group - 1, HD:MSG, :]

        @pl.when(g < groups - 1)
        def _():
            copy2().start()

    def exchange_prefix():
        @pl.when(g > 0)
        def _():
            copy2().wait_recv()

        msg3[0] = prev[...]
        for j in range(group - 1):
            before_id = msg3[j, HD : HD + 1, :]
            same = got1[j, HD : HD + 1, :] == before_id
            msg3[j + 1, 0:HD, :] = got1[j, 0:HD, :] + jnp.where(same, msg3[j, 0:HD, :], 0.0)
            msg3[j + 1, HD:MSG, :] = got1[j, HD:MSG, :]
        got3[pl.ds(m, 1)] = msg3[pl.ds(m, 1)]
        for d in range(1, group):
            copy3(d).start()

    w_copies[2].wait()
    s_of = lax.broadcasted_iota(jnp.int32, (CH, CH), 0)
    t_of = lax.broadcasted_iota(jnp.int32, (CH, CH), 1)

    def attend(i, carry):
        @pl.when(i == tiles // 2)
        def _():
            exchange_tail()

        @pl.when(i == tiles - 1)
        def _():
            exchange_prefix()

        rows = pl.ds(pl.multiple_of(i * TILE, TILE), TILE)
        qs[rows, :] = dot(hid[rows, :], wq[...]).astype(BF16)
        for j in range(per):
            c = i * per + j
            part = pl.ds(pl.multiple_of(c * CH, CH), CH)
            col = idc[part, :]
            row = jnp.concatenate(
                [ids[pl.ds(c * (CH // 128) + r, 1), :].astype(F32) for r in range(CH // 128)], axis=1
            )
            keep = (jnp.concatenate([col] * (CH // 128), axis=1) == row) & (t_of <= s_of)
            mask = jnp.where(keep, 1.0, 0.0).astype(BF16)
            old = jnp.where(col == before(c), 1.0, 0.0).astype(BF16)
            for h in range(H):
                lanes = slice(h * HD, (h + 1) * HD)
                q = qs[part, lanes]
                scores = lax.dot_general(
                    q, ks[part, lanes], (((1,), (1,)), ((), ())), preferred_element_type=F32
                )
                scores = scores.astype(BF16) * mask
                loc[part, lanes] = dot(scores, vs[part, lanes]) + dot(q * old, sb[c, h])
        return carry

    lax.fori_loop(0, tiles, attend, 0)

    for d in range(1, group):
        copy3(d).wait_recv()
    for h in range(H):
        cb[h] = got3[h, 0:HD, :].astype(BF16)
    carry_id = got3[0, HD : HD + 1, :]
    w_copies[3].wait()

    def out_copy(i):
        rows = pl.ds(pl.multiple_of(i * TILE, TILE), TILE)
        return pltpu.make_async_copy(outv.at[rows], out_hbm.at[rows], out_sem.at[i])

    def finish(i, carry):
        rows = pl.ds(pl.multiple_of(i * TILE, TILE), TILE)
        old = jnp.where(idc[rows, :] == carry_id, 1.0, 0.0).astype(BF16)
        normed = []
        for h in range(H):
            lanes = slice(h * HD, (h + 1) * HD)
            mixed = loc[rows, lanes] + dot(qs[rows, lanes] * old, cb[h])
            scale = lax.rsqrt(jnp.mean(mixed * mixed, axis=1, keepdims=True) + 1e-6)
            normed.append((mixed * scale * gain[:, lanes]).astype(BF16))
        outv[rows, :] = dot(jnp.concatenate(normed, axis=1), wo[...]).astype(BF16)
        out_copy(i).start()
        return carry

    lax.fori_loop(0, tiles, finish, 0)

    for i in range(tiles):
        out_copy(i).wait()
    for d in range(1, group):
        copy1(d).wait_send()
        copy3(d).wait_send()

    @pl.when(g < groups - 1)
    def _():
        copy2().wait_send()


def body(n_outer, n_inner, hidden, segment_ids, wq, wk, wv, wo, gain):
    tokens = hidden.shape[0]
    group = MOST_LEN // tokens
    chunks = tokens // CH
    vm = pl.BlockSpec(memory_space=pltpu.VMEM)
    hbm = pl.BlockSpec(memory_space=pl.ANY)
    dma = pltpu.SemaphoreType.DMA
    weight = pltpu.VMEM((D, D), BF16)
    wide = pltpu.VMEM((tokens, D), BF16)
    msgs = pltpu.VMEM((group, MSG, HD), F32)
    one = pltpu.VMEM((MSG, HD), F32)
    call = pl.pallas_call(
        functools.partial(kernel, n_outer, n_inner, group),
        out_shape=jax.ShapeDtypeStruct((tokens, D), BF16),
        in_specs=[vm, vm, hbm, hbm, hbm, hbm, hbm],
        out_specs=hbm,
        scratch_shapes=[
            wide, weight, weight, weight, weight, wide, wide, wide,
            pltpu.VMEM((tokens, D), F32), wide,
            pltpu.VMEM((tokens, 128), F32),
            pltpu.VMEM((H, HD, HD), F32),
            pltpu.VMEM((chunks, H, HD, HD), BF16),
            pltpu.VMEM((H, HD, HD), BF16),
            msgs, msgs, one, one, msgs, msgs,
            dma((tokens // TILE,)), dma((4,)), dma((tokens // TILE,)),
            dma((group - 1,)), dma((group - 1,)), dma, dma, dma((group - 1,)), dma((group - 1,)),
        ],
        compiler_params=pltpu.CompilerParams(
            collective_id=0, has_side_effects=True, vmem_limit_bytes=58 * 1024 * 1024
        ),
        cost_estimate=pl.CostEstimate(flops=22 * 10**9, bytes_accessed=16 * 2**20, transcendentals=0),
    )
    return call(
        segment_ids.reshape(tokens // 128, 128), gain.reshape(1, D), hidden, wq, wk, wv, wo
    )


def solution(mesh):
    both = ("outer", "inner")
    in_specs = (P(both, None), P(both), P(), P(), P(), P(), P())
    run = functools.partial(body, mesh.shape["outer"], mesh.shape["inner"])
    return jax.shard_map(run, mesh=mesh, in_specs=in_specs, out_specs=P(both, None), check_vma=False)
```

```python
import functools

import jax
import jax.numpy as jnp
from jax import lax
from jax.experimental import pallas as pl
from jax.experimental.pallas import tpu as pltpu
from jax.sharding import PartitionSpec as P

D = 1024
H = 8
HD = 128
MOST_LEN = 16384
TILE = 512
CH = 256
LAST = 256
MSG = HD + 8
MESH = pl.DeviceIdType.MESH
F32 = jnp.float32
BF16 = jnp.bfloat16


def dot(a, b):
    return jnp.dot(a, b, preferred_element_type=F32)


def column(ids_row):
    return jnp.transpose(jnp.broadcast_to(ids_row.astype(F32), (128, 128)))


def kernel(
    n_outer, n_inner, group,
    ids, hid_hbm, wq_hbm, wk_hbm, wv_hbm, q_hbm, loc_hbm, carry, carry_id,
    hid, wq, wk, wv, qs, ks, vs, loc, idc, sb,
    msg1, got1, tail, prev, msg3, got3,
    hid_sem, w_sem, q_sem, loc_sem, s1, r1, s2, r2, s3, r3,
):
    tokens = hid.shape[0]
    tiles = tokens // TILE
    per = TILE // CH
    total = n_outer * n_inner
    groups = total // group
    half = H // 2
    me = lax.axis_index("outer") * n_inner + lax.axis_index("inner")
    g = me // group
    m = me % group
    parity = m % 2
    mine = parity * half + m // 2

    def at(index):
        return (index // n_inner, index % n_inner)

    def peer(d):
        return (m + d) % group

    def rows_of(i):
        return pl.ds(pl.multiple_of(i * TILE, TILE), TILE)

    def hid_copy(i):
        return pltpu.make_async_copy(hid_hbm.at[rows_of(i)], hid.at[rows_of(i)], hid_sem.at[i])

    def half_copies(p):
        cols = slice(p * half * HD, (p + 1) * half * HD)
        return (
            pltpu.make_async_copy(wk_hbm.at[:, cols], wk.at[:, cols], w_sem.at[2 * p]),
            pltpu.make_async_copy(wv_hbm.at[:, cols], wv.at[:, cols], w_sem.at[2 * p + 1]),
        )

    wq_copy = pltpu.make_async_copy(wq_hbm, wq, w_sem.at[4])
    first = half_copies(0)
    first[0].start()
    hid_copy(0).start()
    first[1].start()
    for i in range(1, tiles):
        hid_copy(i).start()
    for copy in half_copies(1):
        copy.start()
    wq_copy.start()

    barrier = pltpu.get_barrier_semaphore()
    for d in range(1, group):
        pl.semaphore_signal(barrier, inc=1, device_id=at(g * group + peer(d)), device_id_type=MESH)

    @pl.when(g > 0)
    def _():
        pl.semaphore_signal(barrier, inc=1, device_id=at(me - group), device_id_type=MESH)

    @pl.when(g < groups - 1)
    def _():
        pl.semaphore_signal(barrier, inc=1, device_id=at(me + group), device_id_type=MESH)

    for r in range(tokens // 128):
        idc[r * 128 : (r + 1) * 128, :] = column(ids[r : r + 1, :])

    def last_of(c):
        return idc[pl.ds(pl.multiple_of(c * CH + CH - 8, 8), 8), :][7:8, :]

    def before(c):
        return idc[pl.ds(pl.multiple_of(jnp.maximum(c * CH - 8, 0), 8), 8), :][7:8, :]

    my_last = jnp.broadcast_to(last_of(tokens // CH - 1), (8, 128))
    for h in range(H):
        msg1[h, 0:HD, :] = jnp.zeros((HD, HD), F32)
        msg1[h, HD:MSG, :] = my_last

    @pl.when(g == 0)
    def _():
        prev[0:HD, :] = jnp.zeros((HD, HD), F32)
        prev[HD:MSG, :] = jnp.full((8, HD), -1.0, F32)

    def copy1(d):
        to = peer(d)
        return pltpu.make_async_remote_copy(
            src_ref=msg1.at[(to % 2) * half + to // 2], dst_ref=got1.at[m],
            send_sem=s1.at[d], recv_sem=r1.at[d],
            device_id=at(g * group + to), device_id_type=MESH,
        )

    def copy2():
        return pltpu.make_async_remote_copy(
            src_ref=tail, dst_ref=prev, send_sem=s2, recv_sem=r2,
            device_id=at(me + group), device_id_type=MESH,
        )

    def copy3(d):
        return pltpu.make_async_remote_copy(
            src_ref=msg3.at[peer(d)], dst_ref=got3.at[mine],
            send_sem=s3.at[d], recv_sem=r3.at[d],
            device_id=at(g * group + peer(d)), device_id_type=MESH,
        )

    def send_half(p):
        odd = (parity + p) % 2
        for k in range(group // 2):
            if k > 0:
                copy1(2 * k + odd).start()
            else:
                @pl.when(odd == 1)
                def _():
                    copy1(1).start()

                @pl.when(odd == 0)
                def _():
                    got1[pl.ds(m, 1)] = msg1[pl.ds(mine, 1)]

    def exchange_tail():
        for d in range(1, group):
            copy1(d).wait_recv()
        state = got1[0, 0:HD, :]
        for j in range(1, group):
            same = got1[j, HD : HD + 1, :] == got1[j - 1, HD : HD + 1, :]
            state = got1[j, 0:HD, :] + jnp.where(same, state, 0.0)
        tail[0:HD, :] = state
        tail[HD:MSG, :] = got1[group - 1, HD:MSG, :]

        @pl.when(g < groups - 1)
        def _():
            copy2().start()

    def exchange_prefix():
        @pl.when(g > 0)
        def _():
            copy2().wait_recv()

        msg3[0] = prev[...]
        for j in range(group - 1):
            before_id = msg3[j, HD : HD + 1, :]
            same = got1[j, HD : HD + 1, :] == before_id
            msg3[j + 1, 0:HD, :] = got1[j, 0:HD, :] + jnp.where(same, msg3[j, 0:HD, :], 0.0)
            msg3[j + 1, HD:MSG, :] = got1[j, HD:MSG, :]
        got3[pl.ds(mine, 1)] = msg3[pl.ds(m, 1)]
        for d in range(1, group):
            copy3(d).start()

    def project(p):
        cols = slice(p * half * HD, (p + 1) * half * HD)

        def tile(i, unused):
            if p == 0:
                hid_copy(i).wait()
            rows = rows_of(i)
            x = hid[rows, :]
            ks[rows, cols] = dot(x, wk[:, cols]).astype(BF16)
            vs[rows, cols] = dot(x, wv[:, cols]).astype(BF16)
            for j in range(per):
                c = i * per + j
                part = pl.ds(pl.multiple_of(c * CH, CH), CH)
                last = last_of(c)
                held = last == before(c)
                mask = jnp.where(idc[part, :] == last, 1.0, 0.0).astype(BF16)
                for h in range(p * half, (p + 1) * half):
                    lanes = slice(h * HD, (h + 1) * HD)
                    state = msg1[h, 0:HD, :]
                    sb[c, h] = state.astype(BF16)
                    add = lax.dot_general(
                        ks[part, lanes] * mask, vs[part, lanes], (((0,), (0,)), ((), ())),
                        preferred_element_type=F32,
                    )
                    msg1[h, 0:HD, :] = jnp.where(held, state, 0.0) + add
            return unused

        for copy in half_copies(p):
            copy.wait()
        lax.fori_loop(0, tiles, tile, 0)

    project(0)
    has_prev = jnp.where(g > 0, 1, 0)
    has_next = jnp.where(g < groups - 1, 1, 0)
    pl.semaphore_wait(barrier, group - 1 + has_prev + has_next)
    send_half(0)
    project(1)
    send_half(1)

    @pl.when(parity == 0)
    def _():
        exchange_tail()

    wq_copy.wait()
    s_of = lax.broadcasted_iota(jnp.int32, (CH, CH), 0)
    t_of = lax.broadcasted_iota(jnp.int32, (CH, CH), 1)

    def q_copy(i):
        return pltpu.make_async_copy(qs.at[rows_of(i)], q_hbm.at[rows_of(i)], q_sem.at[i])

    def loc_copy(i):
        return pltpu.make_async_copy(loc.at[rows_of(i)], loc_hbm.at[rows_of(i)], loc_sem.at[i])

    def attend(i, unused):
        @pl.when((i == 1) & (parity == 0))
        def _():
            exchange_prefix()

        rows = rows_of(i)
        qs[rows, :] = dot(hid[rows, :], wq[...]).astype(BF16)

        @pl.when((i == 1) & (parity == 1))
        def _():
            exchange_tail()

        @pl.when((i == 2) & (parity == 1))
        def _():
            exchange_prefix()

        for j in range(per):
            c = i * per + j
            part = pl.ds(pl.multiple_of(c * CH, CH), CH)
            col = idc[part, :]
            row = jnp.concatenate(
                [ids[pl.ds(c * (CH // 128) + r, 1), :].astype(F32) for r in range(CH // 128)], axis=1
            )
            keep = (jnp.concatenate([col] * (CH // 128), axis=1) == row) & (t_of <= s_of)
            mask = jnp.where(keep, 1.0, 0.0).astype(BF16)
            old = jnp.where(col == before(c), 1.0, 0.0).astype(BF16)
            for h in range(H):
                lanes = slice(h * HD, (h + 1) * HD)
                q = qs[part, lanes]
                scores = lax.dot_general(
                    q, ks[part, lanes], (((1,), (1,)), ((), ())), preferred_element_type=F32
                )
                scores = scores.astype(BF16) * mask
                mixed = dot(scores, vs[part, lanes]) + dot(q * old, sb[c, h])
                loc[part, lanes] = mixed.astype(BF16)
        q_copy(i).start()
        loc_copy(i).start()
        return unused

    lax.fori_loop(0, tiles, attend, 0)

    for d in range(1, group):
        copy3(d).wait_recv()
    for h in range(H):
        carry[h] = got3[h, 0:HD, :].astype(BF16)
    carry_id[...] = got3[0, HD:MSG, :]

    for d in range(1, group):
        copy1(d).wait_send()
        copy3(d).wait_send()

    @pl.when(g < groups - 1)
    def _():
        copy2().wait_send()

    for i in range(tiles):
        q_copy(i).wait()
        loc_copy(i).wait()


def finish(ids, carry_id, gain, carry, q_ref, loc_ref, wo, out):
    tile = q_ref.shape[0]
    steps = tile // 128
    first = pl.program_id(0) * steps
    col = jnp.concatenate([column(ids[pl.ds(first + r, 1), :]) for r in range(steps)], axis=0)
    old = jnp.where(col == carry_id[0:1, :], 1.0, 0.0).astype(BF16)
    normed = []
    for h in range(H):
        lanes = slice(h * HD, (h + 1) * HD)
        mixed = loc_ref[:, lanes].astype(F32) + dot(q_ref[:, lanes] * old, carry[h])
        scale = lax.rsqrt(jnp.mean(mixed * mixed, axis=1, keepdims=True) + 1e-6)
        normed.append((mixed * scale * gain[:, lanes]).astype(BF16))
    out[...] = dot(jnp.concatenate(normed, axis=1), wo[...]).astype(BF16)


def body(n_outer, n_inner, hidden, segment_ids, wq, wk, wv, wo, gain):
    tokens = hidden.shape[0]
    group = MOST_LEN // tokens
    chunks = tokens // CH
    vm = pl.BlockSpec(memory_space=pltpu.VMEM)
    hbm = pl.BlockSpec(memory_space=pl.ANY)
    dma = pltpu.SemaphoreType.DMA
    weight = pltpu.VMEM((D, D), BF16)
    wide = pltpu.VMEM((tokens, D), BF16)
    msgs = pltpu.VMEM((group, MSG, HD), F32)
    one = pltpu.VMEM((MSG, HD), F32)
    ids = segment_ids.reshape(tokens // 128, 128)
    tiles = tokens // TILE
    local = pl.pallas_call(
        functools.partial(kernel, n_outer, n_inner, group),
        out_shape=[
            jax.ShapeDtypeStruct((tokens, D), BF16),
            jax.ShapeDtypeStruct((tokens, D), BF16),
            jax.ShapeDtypeStruct((H, HD, HD), BF16),
            jax.ShapeDtypeStruct((8, HD), F32),
        ],
        in_specs=[vm, hbm, hbm, hbm, hbm],
        out_specs=[hbm, hbm, vm, vm],
        scratch_shapes=[
            wide, weight, weight, weight, wide, wide, wide, wide,
            pltpu.VMEM((tokens, 128), F32),
            pltpu.VMEM((chunks, H, HD, HD), BF16),
            msgs, msgs, one, one, msgs, msgs,
            dma((tiles,)), dma((5,)), dma((tiles,)), dma((tiles,)),
            dma((group,)), dma((group,)), dma, dma, dma((group,)), dma((group,)),
        ],
        compiler_params=pltpu.CompilerParams(
            collective_id=0, has_side_effects=True, vmem_limit_bytes=54 * 2**20
        ),
        cost_estimate=pl.CostEstimate(flops=17 * 10**9, bytes_accessed=18 * 2**20, transcendentals=0),
    )
    queries, mixed, carry, carry_id = local(ids, hidden, wq, wk, wv)

    def whole(shape):
        return pl.BlockSpec(shape, lambda i: (0,) * len(shape))

    step = pl.BlockSpec((LAST, D), lambda i: (i, 0))
    return pl.pallas_call(
        finish,
        grid=(tokens // LAST,),
        out_shape=jax.ShapeDtypeStruct((tokens, D), BF16),
        in_specs=[
            whole(ids.shape), whole((8, HD)), whole((1, D)), whole((H, HD, HD)), step, step, whole((D, D)),
        ],
        out_specs=step,
        compiler_params=pltpu.CompilerParams(vmem_limit_bytes=58 * 2**20),
        cost_estimate=pl.CostEstimate(flops=5 * 10**9, bytes_accessed=14 * 2**20, transcendentals=0),
    )(ids, carry_id, gain.reshape(1, D), carry, queries, mixed, wo)


def solution(mesh):
    both = ("outer", "inner")
    in_specs = (P(both, None), P(both), P(), P(), P(), P(), P())
    run = functools.partial(body, mesh.shape["outer"], mesh.shape["inner"])
    return jax.shard_map(run, mesh=mesh, in_specs=in_specs, out_specs=P(both, None), check_vma=False)
```

```python
import functools

import jax
import jax.numpy as jnp
from jax import lax
from jax.experimental import pallas as pl
from jax.experimental.pallas import tpu as pltpu
from jax.sharding import PartitionSpec as P

D = 1024
H = 8
HD = 128
MOST_LEN = 16384
TILE = 512
CH = 256
LAST = 512
MSG = HD + 8
MESH = pl.DeviceIdType.MESH
F32 = jnp.float32
BF16 = jnp.bfloat16


def dot(a, b):
    return jnp.dot(a, b, preferred_element_type=F32)


def column(ids_row):
    return jnp.transpose(jnp.broadcast_to(ids_row.astype(F32), (128, 128)))


def kernel(
    n_outer, n_inner, group,
    ids, hid_hbm, wq_hbm, wk_hbm, wv_hbm, q_hbm, loc_hbm, carry, carry_id,
    hid, wq, wk, wv, qs, ks, vs, loc, idc, sb,
    msg1, got1, tail, prev, msg3, got3,
    hid_sem, w_sem, q_sem, loc_sem, s1, r1, s2, r2, s3, r3,
):
    tokens = hid.shape[0]
    tiles = tokens // TILE
    per = TILE // CH
    total = n_outer * n_inner
    groups = total // group
    half = H // 2
    me = lax.axis_index("outer") * n_inner + lax.axis_index("inner")
    g = me // group
    m = me % group
    parity = m % 2
    mine = parity * half + m // 2

    def at(index):
        return (index // n_inner, index % n_inner)

    def peer(d):
        return (m + d) % group

    def rows_of(i):
        return pl.ds(pl.multiple_of(i * TILE, TILE), TILE)

    def hid_copy(i):
        return pltpu.make_async_copy(hid_hbm.at[rows_of(i)], hid.at[rows_of(i)], hid_sem.at[i])

    def half_copies(p):
        cols = slice(p * half * HD, (p + 1) * half * HD)
        return (
            pltpu.make_async_copy(wk_hbm.at[:, cols], wk.at[:, cols], w_sem.at[2 * p]),
            pltpu.make_async_copy(wv_hbm.at[:, cols], wv.at[:, cols], w_sem.at[2 * p + 1]),
        )

    wq_copy = pltpu.make_async_copy(wq_hbm, wq, w_sem.at[4])
    first = half_copies(0)
    first[0].start()
    hid_copy(0).start()
    first[1].start()
    for i in range(1, tiles):
        hid_copy(i).start()
    for copy in half_copies(1):
        copy.start()
    wq_copy.start()

    barrier = pltpu.get_barrier_semaphore()
    for d in range(1, group):
        pl.semaphore_signal(barrier, inc=1, device_id=at(g * group + peer(d)), device_id_type=MESH)

    @pl.when(g > 0)
    def _():
        pl.semaphore_signal(barrier, inc=1, device_id=at(me - group), device_id_type=MESH)

    @pl.when(g < groups - 1)
    def _():
        pl.semaphore_signal(barrier, inc=1, device_id=at(me + group), device_id_type=MESH)

    for r in range(tokens // 128):
        idc[r * 128 : (r + 1) * 128, :] = column(ids[r : r + 1, :])

    def last_of(c):
        return idc[pl.ds(pl.multiple_of(c * CH + CH - 8, 8), 8), :][7:8, :]

    def before(c):
        return idc[pl.ds(pl.multiple_of(jnp.maximum(c * CH - 8, 0), 8), 8), :][7:8, :]

    my_last = jnp.broadcast_to(last_of(tokens // CH - 1), (8, 128))
    for h in range(H):
        msg1[h, 0:HD, :] = jnp.zeros((HD, HD), F32)
        msg1[h, HD:MSG, :] = my_last

    @pl.when(g == 0)
    def _():
        prev[0:HD, :] = jnp.zeros((HD, HD), F32)
        prev[HD:MSG, :] = jnp.full((8, HD), -1.0, F32)

    def copy1(d):
        to = peer(d)
        return pltpu.make_async_remote_copy(
            src_ref=msg1.at[(to % 2) * half + to // 2], dst_ref=got1.at[m],
            send_sem=s1.at[d], recv_sem=r1.at[d],
            device_id=at(g * group + to), device_id_type=MESH,
        )

    def copy2():
        return pltpu.make_async_remote_copy(
            src_ref=tail, dst_ref=prev, send_sem=s2, recv_sem=r2,
            device_id=at(me + group), device_id_type=MESH,
        )

    def copy3(d):
        return pltpu.make_async_remote_copy(
            src_ref=msg3.at[peer(d)], dst_ref=got3.at[mine],
            send_sem=s3.at[d], recv_sem=r3.at[d],
            device_id=at(g * group + peer(d)), device_id_type=MESH,
        )

    def send_half(p):
        odd = (parity + p) % 2
        for k in range(group // 2):
            if k > 0:
                copy1(2 * k + odd).start()
            else:
                @pl.when(odd == 1)
                def _():
                    copy1(1).start()

                @pl.when(odd == 0)
                def _():
                    got1[pl.ds(m, 1)] = msg1[pl.ds(mine, 1)]

    def exchange_tail():
        for d in range(1, group):
            copy1(d).wait_recv()
        state = got1[0, 0:HD, :]
        for j in range(1, group):
            same = got1[j, HD : HD + 1, :] == got1[j - 1, HD : HD + 1, :]
            state = got1[j, 0:HD, :] + jnp.where(same, state, 0.0)
        tail[0:HD, :] = state
        tail[HD:MSG, :] = got1[group - 1, HD:MSG, :]

        @pl.when(g < groups - 1)
        def _():
            copy2().start()

    def exchange_prefix():
        @pl.when(g > 0)
        def _():
            copy2().wait_recv()

        msg3[0] = prev[...]
        for j in range(group - 1):
            before_id = msg3[j, HD : HD + 1, :]
            same = got1[j, HD : HD + 1, :] == before_id
            msg3[j + 1, 0:HD, :] = got1[j, 0:HD, :] + jnp.where(same, msg3[j, 0:HD, :], 0.0)
            msg3[j + 1, HD:MSG, :] = got1[j, HD:MSG, :]
        got3[pl.ds(mine, 1)] = msg3[pl.ds(m, 1)]
        for d in range(1, group):
            copy3(d).start()

    def project(p):
        cols = slice(p * half * HD, (p + 1) * half * HD)

        def tile(i, unused):
            if p == 0:
                hid_copy(i).wait()
            rows = rows_of(i)
            x = hid[rows, :]
            ks[rows, cols] = dot(x, wk[:, cols]).astype(BF16)
            vs[rows, cols] = dot(x, wv[:, cols]).astype(BF16)
            for j in range(per):
                c = i * per + j
                part = pl.ds(pl.multiple_of(c * CH, CH), CH)
                last = last_of(c)
                held = last == before(c)
                mask = jnp.where(idc[part, :] == last, 1.0, 0.0).astype(BF16)
                for h in range(p * half, (p + 1) * half):
                    lanes = slice(h * HD, (h + 1) * HD)
                    state = msg1[h, 0:HD, :]
                    sb[c, h] = state.astype(BF16)
                    add = lax.dot_general(
                        ks[part, lanes] * mask, vs[part, lanes], (((0,), (0,)), ((), ())),
                        preferred_element_type=F32,
                    )
                    msg1[h, 0:HD, :] = jnp.where(held, state, 0.0) + add
            return unused

        for copy in half_copies(p):
            copy.wait()
        lax.fori_loop(0, tiles, tile, 0)

    project(0)
    has_prev = jnp.where(g > 0, 1, 0)
    has_next = jnp.where(g < groups - 1, 1, 0)
    pl.semaphore_wait(barrier, group - 1 + has_prev + has_next)
    send_half(0)
    project(1)
    send_half(1)

    @pl.when(parity == 0)
    def _():
        exchange_tail()

    wq_copy.wait()
    s_of = lax.broadcasted_iota(jnp.int32, (CH, CH), 0)
    t_of = lax.broadcasted_iota(jnp.int32, (CH, CH), 1)

    def q_copy(i):
        return pltpu.make_async_copy(qs.at[rows_of(i)], q_hbm.at[rows_of(i)], q_sem.at[i])

    def loc_copy(i):
        return pltpu.make_async_copy(loc.at[rows_of(i)], loc_hbm.at[rows_of(i)], loc_sem.at[i])

    def attend(i, unused):
        @pl.when((i == 1) & (parity == 0))
        def _():
            exchange_prefix()

        rows = rows_of(i)
        qs[rows, :] = dot(hid[rows, :], wq[...]).astype(BF16)

        @pl.when((i == 1) & (parity == 1))
        def _():
            exchange_tail()

        @pl.when((i == 2) & (parity == 1))
        def _():
            exchange_prefix()

        for j in range(per):
            c = i * per + j
            part = pl.ds(pl.multiple_of(c * CH, CH), CH)
            col = idc[part, :]
            row = jnp.concatenate(
                [ids[pl.ds(c * (CH // 128) + r, 1), :].astype(F32) for r in range(CH // 128)], axis=1
            )
            keep = (jnp.concatenate([col] * (CH // 128), axis=1) == row) & (t_of <= s_of)
            mask = jnp.where(keep, 1.0, 0.0).astype(BF16)
            old = jnp.where(col == before(c), 1.0, 0.0).astype(BF16)
            for h in range(H):
                lanes = slice(h * HD, (h + 1) * HD)
                q = qs[part, lanes]
                scores = lax.dot_general(
                    q, ks[part, lanes], (((1,), (1,)), ((), ())), preferred_element_type=F32
                )
                scores = scores.astype(BF16) * mask
                mixed = dot(scores, vs[part, lanes]) + dot(q * old, sb[c, h])
                loc[part, lanes] = mixed.astype(BF16)
        q_copy(i).start()
        loc_copy(i).start()
        return unused

    lax.fori_loop(0, tiles, attend, 0)

    for d in range(1, group):
        copy3(d).wait_recv()
    for h in range(H):
        carry[h] = got3[h, 0:HD, :].astype(BF16)
    carry_id[...] = got3[0, HD:MSG, :]

    for d in range(1, group):
        copy1(d).wait_send()
        copy3(d).wait_send()

    @pl.when(g < groups - 1)
    def _():
        copy2().wait_send()

    for i in range(tiles):
        q_copy(i).wait()
        loc_copy(i).wait()


def finish(ids, carry_id, gain, carry, q_ref, loc_ref, wo, out):
    tile = q_ref.shape[0]
    steps = tile // 128
    first = pl.program_id(0) * steps
    col = jnp.concatenate([column(ids[pl.ds(first + r, 1), :]) for r in range(steps)], axis=0)
    old = jnp.where(col == carry_id[0:1, :], 1.0, 0.0).astype(BF16)
    pair = 2 * HD
    r_head = lax.broadcasted_iota(jnp.int32, (pair, pair), 0) // HD
    c_head = lax.broadcasted_iota(jnp.int32, (pair, pair), 1) // HD
    average = jnp.where(r_head == c_head, 1.0 / HD, 0.0).astype(BF16)
    normed = []
    for p in range(H // 2):
        lanes = slice(p * pair, (p + 1) * pair)
        carried = [
            dot(q_ref[:, h * HD : (h + 1) * HD] * old, carry[h]) for h in (2 * p, 2 * p + 1)
        ]
        mixed = loc_ref[:, lanes].astype(F32) + jnp.concatenate(carried, axis=1)
        scale = lax.rsqrt(dot((mixed * mixed).astype(BF16), average) + 1e-6)
        normed.append((mixed * scale * gain[:, lanes]).astype(BF16))
    out[...] = dot(jnp.concatenate(normed, axis=1), wo[...]).astype(BF16)


def body(n_outer, n_inner, hidden, segment_ids, wq, wk, wv, wo, gain):
    tokens = hidden.shape[0]
    group = MOST_LEN // tokens
    chunks = tokens // CH
    vm = pl.BlockSpec(memory_space=pltpu.VMEM)
    hbm = pl.BlockSpec(memory_space=pl.ANY)
    dma = pltpu.SemaphoreType.DMA
    weight = pltpu.VMEM((D, D), BF16)
    wide = pltpu.VMEM((tokens, D), BF16)
    msgs = pltpu.VMEM((group, MSG, HD), F32)
    one = pltpu.VMEM((MSG, HD), F32)
    ids = segment_ids.reshape(tokens // 128, 128)
    tiles = tokens // TILE
    local = pl.pallas_call(
        functools.partial(kernel, n_outer, n_inner, group),
        out_shape=[
            jax.ShapeDtypeStruct((tokens, D), BF16),
            jax.ShapeDtypeStruct((tokens, D), BF16),
            jax.ShapeDtypeStruct((H, HD, HD), BF16),
            jax.ShapeDtypeStruct((8, HD), F32),
        ],
        in_specs=[vm, hbm, hbm, hbm, hbm],
        out_specs=[hbm, hbm, vm, vm],
        scratch_shapes=[
            wide, weight, weight, weight, wide, wide, wide, wide,
            pltpu.VMEM((tokens, 128), F32),
            pltpu.VMEM((chunks, H, HD, HD), BF16),
            msgs, msgs, one, one, msgs, msgs,
            dma((tiles,)), dma((5,)), dma((tiles,)), dma((tiles,)),
            dma((group,)), dma((group,)), dma, dma, dma((group,)), dma((group,)),
        ],
        compiler_params=pltpu.CompilerParams(
            collective_id=0, has_side_effects=True, vmem_limit_bytes=54 * 2**20
        ),
        cost_estimate=pl.CostEstimate(flops=17 * 10**9, bytes_accessed=18 * 2**20, transcendentals=0),
    )
    queries, mixed, carry, carry_id = local(ids, hidden, wq, wk, wv)

    def whole(shape):
        return pl.BlockSpec(shape, lambda i: (0,) * len(shape))

    step = pl.BlockSpec((LAST, D), lambda i: (i, 0))
    return pl.pallas_call(
        finish,
        grid=(tokens // LAST,),
        out_shape=jax.ShapeDtypeStruct((tokens, D), BF16),
        in_specs=[
            whole(ids.shape), whole((8, HD)), whole((1, D)), whole((H, HD, HD)), step, step, whole((D, D)),
        ],
        out_specs=step,
        compiler_params=pltpu.CompilerParams(vmem_limit_bytes=58 * 2**20),
        cost_estimate=pl.CostEstimate(flops=5 * 10**9, bytes_accessed=14 * 2**20, transcendentals=0),
    )(ids, carry_id, gain.reshape(1, D), carry, queries, mixed, wo)


def solution(mesh):
    both = ("outer", "inner")
    in_specs = (P(both, None), P(both), P(), P(), P(), P(), P())
    run = functools.partial(body, mesh.shape["outer"], mesh.shape["inner"])
    return jax.shard_map(run, mesh=mesh, in_specs=in_specs, out_specs=P(both, None), check_vma=False)
```

```python
import functools

import jax
import jax.numpy as jnp
from jax import lax
from jax.experimental import pallas as pl
from jax.experimental.pallas import tpu as pltpu
from jax.sharding import PartitionSpec as P

D = 1024
H = 8
HD = 128
MOST_LEN = 16384
TILE = 512
CH = 128
LAST = 512
MSG = HD + 8
MESH = pl.DeviceIdType.MESH
F32 = jnp.float32
BF16 = jnp.bfloat16


def dot(a, b):
    return jnp.dot(a, b, preferred_element_type=F32)


def column(ids_row):
    return jnp.transpose(jnp.broadcast_to(ids_row.astype(F32), (128, 128)))


def kernel(
    n_outer, n_inner, group,
    ids, hid_hbm, wq_hbm, wk_hbm, wv_hbm, q_hbm, loc_hbm, carry, carry_id,
    hid, wq, wk, wv, qs, ks, vs, loc, idc, sb,
    msg1, got1, tail, prev, msg3, got3,
    hid_sem, w_sem, q_sem, loc_sem, s1, r1, s2, r2, s3, r3,
):
    tokens = hid.shape[0]
    tiles = tokens // TILE
    per = TILE // CH
    total = n_outer * n_inner
    groups = total // group
    half = H // 2
    me = lax.axis_index("outer") * n_inner + lax.axis_index("inner")
    g = me // group
    m = me % group
    parity = m % 2
    mine = parity * half + m // 2

    def at(index):
        return (index // n_inner, index % n_inner)

    def peer(d):
        return (m + d) % group

    def rows_of(i):
        return pl.ds(pl.multiple_of(i * TILE, TILE), TILE)

    def hid_copy(i):
        return pltpu.make_async_copy(hid_hbm.at[rows_of(i)], hid.at[rows_of(i)], hid_sem.at[i])

    def half_copies(p):
        cols = slice(p * half * HD, (p + 1) * half * HD)
        return (
            pltpu.make_async_copy(wk_hbm.at[:, cols], wk.at[:, cols], w_sem.at[2 * p]),
            pltpu.make_async_copy(wv_hbm.at[:, cols], wv.at[:, cols], w_sem.at[2 * p + 1]),
        )

    wq_copy = pltpu.make_async_copy(wq_hbm, wq, w_sem.at[4])
    first = half_copies(0)
    first[0].start()
    hid_copy(0).start()
    first[1].start()
    for i in range(1, tiles):
        hid_copy(i).start()
    for copy in half_copies(1):
        copy.start()
    wq_copy.start()

    barrier = pltpu.get_barrier_semaphore()
    for d in range(1, group):
        pl.semaphore_signal(barrier, inc=1, device_id=at(g * group + peer(d)), device_id_type=MESH)

    @pl.when(g > 0)
    def _():
        pl.semaphore_signal(barrier, inc=1, device_id=at(me - group), device_id_type=MESH)

    @pl.when(g < groups - 1)
    def _():
        pl.semaphore_signal(barrier, inc=1, device_id=at(me + group), device_id_type=MESH)

    for r in range(tokens // 128):
        idc[r * 128 : (r + 1) * 128, :] = column(ids[r : r + 1, :])

    def last_of(c):
        return idc[pl.ds(pl.multiple_of(c * CH + CH - 8, 8), 8), :][7:8, :]

    def before(c):
        return idc[pl.ds(pl.multiple_of(jnp.maximum(c * CH - 8, 0), 8), 8), :][7:8, :]

    my_last = jnp.broadcast_to(last_of(tokens // CH - 1), (8, 128))
    for h in range(H):
        msg1[h, 0:HD, :] = jnp.zeros((HD, HD), F32)
        msg1[h, HD:MSG, :] = my_last

    @pl.when(g == 0)
    def _():
        prev[0:HD, :] = jnp.zeros((HD, HD), F32)
        prev[HD:MSG, :] = jnp.full((8, HD), -1.0, F32)

    def copy1(d):
        to = peer(d)
        return pltpu.make_async_remote_copy(
            src_ref=msg1.at[(to % 2) * half + to // 2], dst_ref=got1.at[m],
            send_sem=s1.at[d], recv_sem=r1.at[d],
            device_id=at(g * group + to), device_id_type=MESH,
        )

    def copy2():
        return pltpu.make_async_remote_copy(
            src_ref=tail, dst_ref=prev, send_sem=s2, recv_sem=r2,
            device_id=at(me + group), device_id_type=MESH,
        )

    def copy3(d):
        return pltpu.make_async_remote_copy(
            src_ref=msg3.at[peer(d)], dst_ref=got3.at[mine],
            send_sem=s3.at[d], recv_sem=r3.at[d],
            device_id=at(g * group + peer(d)), device_id_type=MESH,
        )

    def send_half(p):
        odd = (parity + p) % 2
        for k in range(group // 2):
            if k > 0:
                copy1(2 * k + odd).start()
            else:
                @pl.when(odd == 1)
                def _():
                    copy1(1).start()

                @pl.when(odd == 0)
                def _():
                    got1[pl.ds(m, 1)] = msg1[pl.ds(mine, 1)]

    def exchange_tail():
        for d in range(1, group):
            copy1(d).wait_recv()
        state = got1[0, 0:HD, :]
        for j in range(1, group):
            same = got1[j, HD : HD + 1, :] == got1[j - 1, HD : HD + 1, :]
            state = got1[j, 0:HD, :] + jnp.where(same, state, 0.0)
        tail[0:HD, :] = state
        tail[HD:MSG, :] = got1[group - 1, HD:MSG, :]

        @pl.when(g < groups - 1)
        def _():
            copy2().start()

    def exchange_prefix():
        @pl.when(g > 0)
        def _():
            copy2().wait_recv()

        msg3[0] = prev[...]
        for j in range(group - 1):
            before_id = msg3[j, HD : HD + 1, :]
            same = got1[j, HD : HD + 1, :] == before_id
            msg3[j + 1, 0:HD, :] = got1[j, 0:HD, :] + jnp.where(same, msg3[j, 0:HD, :], 0.0)
            msg3[j + 1, HD:MSG, :] = got1[j, HD:MSG, :]
        got3[pl.ds(mine, 1)] = msg3[pl.ds(m, 1)]
        for d in range(1, group):
            copy3(d).start()

    def project(p):
        cols = slice(p * half * HD, (p + 1) * half * HD)

        def tile(i, unused):
            if p == 0:
                hid_copy(i).wait()
            rows = rows_of(i)
            x = hid[rows, :]
            ks[rows, cols] = dot(x, wk[:, cols]).astype(BF16)
            vs[rows, cols] = dot(x, wv[:, cols]).astype(BF16)
            for j in range(per):
                c = i * per + j
                part = pl.ds(pl.multiple_of(c * CH, CH), CH)
                last = last_of(c)
                held = last == before(c)
                mask = jnp.where(idc[part, :] == last, 1.0, 0.0).astype(BF16)
                for h in range(p * half, (p + 1) * half):
                    lanes = slice(h * HD, (h + 1) * HD)
                    state = msg1[h, 0:HD, :]
                    sb[c, h] = state.astype(BF16)
                    add = lax.dot_general(
                        ks[part, lanes] * mask, vs[part, lanes], (((0,), (0,)), ((), ())),
                        preferred_element_type=F32,
                    )
                    msg1[h, 0:HD, :] = jnp.where(held, state, 0.0) + add
            return unused

        for copy in half_copies(p):
            copy.wait()
        lax.fori_loop(0, tiles, tile, 0)

    project(0)
    has_prev = jnp.where(g > 0, 1, 0)
    has_next = jnp.where(g < groups - 1, 1, 0)
    pl.semaphore_wait(barrier, group - 1 + has_prev + has_next)
    send_half(0)
    project(1)
    send_half(1)

    @pl.when(parity == 0)
    def _():
        exchange_tail()

    wq_copy.wait()
    s_of = lax.broadcasted_iota(jnp.int32, (CH, CH), 0)
    t_of = lax.broadcasted_iota(jnp.int32, (CH, CH), 1)

    def q_copy(i):
        return pltpu.make_async_copy(qs.at[rows_of(i)], q_hbm.at[rows_of(i)], q_sem.at[i])

    def loc_copy(i):
        return pltpu.make_async_copy(loc.at[rows_of(i)], loc_hbm.at[rows_of(i)], loc_sem.at[i])

    def attend(i, unused):
        @pl.when((i == 1) & (parity == 0))
        def _():
            exchange_prefix()

        rows = rows_of(i)
        qs[rows, :] = dot(hid[rows, :], wq[...]).astype(BF16)

        @pl.when((i == 1) & (parity == 1))
        def _():
            exchange_tail()

        @pl.when((i == 2) & (parity == 1))
        def _():
            exchange_prefix()

        for j in range(per):
            c = i * per + j
            part = pl.ds(pl.multiple_of(c * CH, CH), CH)
            col = idc[part, :]
            row = jnp.concatenate(
                [ids[pl.ds(c * (CH // 128) + r, 1), :].astype(F32) for r in range(CH // 128)], axis=1
            )
            keep = (jnp.concatenate([col] * (CH // 128), axis=1) == row) & (t_of <= s_of)
            mask = jnp.where(keep, 1.0, 0.0).astype(BF16)
            old = jnp.where(col == before(c), 1.0, 0.0).astype(BF16)
            for h in range(H):
                lanes = slice(h * HD, (h + 1) * HD)
                q = qs[part, lanes]
                scores = lax.dot_general(
                    q, ks[part, lanes], (((1,), (1,)), ((), ())), preferred_element_type=F32
                )
                scores = scores.astype(BF16) * mask
                mixed = dot(scores, vs[part, lanes]) + dot(q * old, sb[c, h])
                loc[part, lanes] = mixed.astype(BF16)
        q_copy(i).start()
        loc_copy(i).start()
        return unused

    lax.fori_loop(0, tiles, attend, 0)

    for d in range(1, group):
        copy3(d).wait_recv()
    for h in range(H):
        carry[h] = got3[h, 0:HD, :].astype(BF16)
    carry_id[...] = got3[0, HD:MSG, :]

    for d in range(1, group):
        copy1(d).wait_send()
        copy3(d).wait_send()

    @pl.when(g < groups - 1)
    def _():
        copy2().wait_send()

    for i in range(tiles):
        q_copy(i).wait()
        loc_copy(i).wait()


def finish(ids, carry_id, gain, carry, q_ref, loc_ref, wo, out):
    tile = q_ref.shape[0]
    steps = tile // 128
    first = pl.program_id(0) * steps
    col = jnp.concatenate([column(ids[pl.ds(first + r, 1), :]) for r in range(steps)], axis=0)
    old = jnp.where(col == carry_id[0:1, :], 1.0, 0.0).astype(BF16)
    pair = 2 * HD
    r_head = lax.broadcasted_iota(jnp.int32, (pair, pair), 0) // HD
    c_head = lax.broadcasted_iota(jnp.int32, (pair, pair), 1) // HD
    average = jnp.where(r_head == c_head, 1.0 / HD, 0.0).astype(BF16)
    normed = []
    for p in range(H // 2):
        lanes = slice(p * pair, (p + 1) * pair)
        carried = [
            dot(q_ref[:, h * HD : (h + 1) * HD] * old, carry[h]) for h in (2 * p, 2 * p + 1)
        ]
        mixed = loc_ref[:, lanes].astype(F32) + jnp.concatenate(carried, axis=1)
        scale = lax.rsqrt(dot((mixed * mixed).astype(BF16), average) + 1e-6)
        normed.append((mixed * scale * gain[:, lanes]).astype(BF16))
    out[...] = dot(jnp.concatenate(normed, axis=1), wo[...]).astype(BF16)


def body(n_outer, n_inner, hidden, segment_ids, wq, wk, wv, wo, gain):
    tokens = hidden.shape[0]
    group = MOST_LEN // tokens
    chunks = tokens // CH
    vm = pl.BlockSpec(memory_space=pltpu.VMEM)
    hbm = pl.BlockSpec(memory_space=pl.ANY)
    dma = pltpu.SemaphoreType.DMA
    weight = pltpu.VMEM((D, D), BF16)
    wide = pltpu.VMEM((tokens, D), BF16)
    msgs = pltpu.VMEM((group, MSG, HD), F32)
    one = pltpu.VMEM((MSG, HD), F32)
    ids = segment_ids.reshape(tokens // 128, 128)
    tiles = tokens // TILE
    local = pl.pallas_call(
        functools.partial(kernel, n_outer, n_inner, group),
        out_shape=[
            jax.ShapeDtypeStruct((tokens, D), BF16),
            jax.ShapeDtypeStruct((tokens, D), BF16),
            jax.ShapeDtypeStruct((H, HD, HD), BF16),
            jax.ShapeDtypeStruct((8, HD), F32),
        ],
        in_specs=[vm, hbm, hbm, hbm, hbm],
        out_specs=[hbm, hbm, vm, vm],
        scratch_shapes=[
            wide, weight, weight, weight, wide, wide, wide, wide,
            pltpu.VMEM((tokens, 128), F32),
            pltpu.VMEM((chunks, H, HD, HD), BF16),
            msgs, msgs, one, one, msgs, msgs,
            dma((tiles,)), dma((5,)), dma((tiles,)), dma((tiles,)),
            dma((group,)), dma((group,)), dma, dma, dma((group,)), dma((group,)),
        ],
        compiler_params=pltpu.CompilerParams(
            collective_id=0, has_side_effects=True, vmem_limit_bytes=54 * 2**20
        ),
        cost_estimate=pl.CostEstimate(flops=17 * 10**9, bytes_accessed=18 * 2**20, transcendentals=0),
    )
    queries, mixed, carry, carry_id = local(ids, hidden, wq, wk, wv)

    def whole(shape):
        return pl.BlockSpec(shape, lambda i: (0,) * len(shape))

    step = pl.BlockSpec((LAST, D), lambda i: (i, 0))
    return pl.pallas_call(
        finish,
        grid=(tokens // LAST,),
        out_shape=jax.ShapeDtypeStruct((tokens, D), BF16),
        in_specs=[
            whole(ids.shape), whole((8, HD)), whole((1, D)), whole((H, HD, HD)), step, step, whole((D, D)),
        ],
        out_specs=step,
        compiler_params=pltpu.CompilerParams(vmem_limit_bytes=58 * 2**20),
        cost_estimate=pl.CostEstimate(flops=5 * 10**9, bytes_accessed=14 * 2**20, transcendentals=0),
    )(ids, carry_id, gain.reshape(1, D), carry, queries, mixed, wo)


def solution(mesh):
    both = ("outer", "inner")
    in_specs = (P(both, None), P(both), P(), P(), P(), P(), P())
    run = functools.partial(body, mesh.shape["outer"], mesh.shape["inner"])
    return jax.shard_map(run, mesh=mesh, in_specs=in_specs, out_specs=P(both, None), check_vma=False)
```
